32 devices in a mesh: seq: 16 (over z, y, core), ch: 2 (over x).
Axes of the slice: x: 2, y: 2, z: 4, core: 2. Of those that a mesh axis runs over, the one named last changes fastest.
Arguments:
- value_stream: bfloat16 [4096, 4096], P('seq', 'ch'), may hold values from -6 to 6
- first_gate: bfloat16 [4096, 4096], P('seq', 'ch'), may hold values from -6 to 6
- second_gate: bfloat16 [4096, 4096], P('seq', 'ch'), may hold values from -6 to 6
- first_filter: bfloat16 [4096, 4096], P('seq', 'ch'), may hold values from -1 to 1
- second_filter: bfloat16 [4096, 4096], P('seq', 'ch'), may hold values from -1 to 1
- first_skip: float32 [4096], P('ch'), may hold values from -1 to 1
- second_skip: float32 [4096], P('ch'), may hold values from -1 to 1
- out_weight: bfloat16 [4096, 4096], P('ch'), may hold values from -0.09375 to 0.09375
Outputs:
- output: bfloat16 [4096, 4096], P('seq', 'ch')
The draws below stay inside these ranges and needn't reach their ends.
All inputs are finite; a program needn't handle non-finite values.
Results may differ from the reference program's by a relative error of at most 0.019.
Values may be sent and summed in bfloat16 or wider, within the bound.
A program may use at most 128 MiB of HBM per device.

```python
import math
import jax
import jax.numpy as jnp
from jax import lax

D = 4096
TOKENS = 4096
INNER = 64
OUTER = 128
POINTS = 8192


def filter_law(key):
    rate_key, noise_key = jax.random.split(key)
    place = jnp.arange(TOKENS, dtype=jnp.float32)[:, None] / TOKENS
    low_rate = 0.5
    high_rate = TOKENS / 40.0
    noise = jnp.clip(jax.random.normal(noise_key, (TOKENS, D), jnp.float32), -4.0, 4.0)
    rates = jnp.exp(jax.random.uniform(rate_key, (1, D), jnp.float32, math.log(low_rate), math.log(high_rate)))
    envelope = jnp.exp(-rates * place)
    scaling = jnp.sqrt(2.0 * rates / (1.0 - jnp.exp(-2.0 * rates)) / TOKENS)
    return jnp.clip(noise * envelope * scaling, -1.0, 1.0).astype(jnp.bfloat16)


def draw_first_filter(key, part):
    return filter_law(jax.random.fold_in(key, 11))


def draw_second_filter(key, part):
    return filter_law(jax.random.fold_in(key, 29))


def shard_levels(key, shape, cuts, smallest, high):
    def one(position, shards_of):
        heights = jax.random.uniform(jax.random.fold_in(jax.random.fold_in(key, 6), position), (shards_of,), jnp.float32, smallest / len(cuts), high / len(cuts))
        return jnp.repeat(jnp.exp(heights), shape[position] // shards_of).reshape((-1,) + (1,) * (len(shape) - position - 1))

    gain = one(*cuts[0])
    for cut in cuts[1:]:
        gain = gain * one(*cut)
    return gain


def scatter_about(rng, dims, deviation, limit, pieces=(), kind=jnp.bfloat16):
    values = deviation * jax.random.normal(rng, dims, jnp.float32)
    if pieces:
        values = values * shard_levels(rng, dims, pieces, -0.22, 0.18)
    return jnp.clip(values, -limit, limit).astype(kind)


def setup_inputs(seed: int = 0) -> dict:
    arg_keys = jax.random.split(jax.random.key(seed), 9)
    value_stream = scatter_about(arg_keys[0], (TOKENS, D), 1.0, 6.0, ((0, 16), (1, 2)))
    first_gate = scatter_about(arg_keys[1], (TOKENS, D), 1.0, 6.0, ((0, 16), (1, 2)))
    second_gate = scatter_about(arg_keys[2], (TOKENS, D), 1.0, 6.0, ((0, 16), (1, 2)))
    first_filter = draw_first_filter(jax.random.fold_in(arg_keys[8], 71), 0)
    second_filter = draw_second_filter(jax.random.fold_in(arg_keys[8], 71), 0)
    first_skip = jnp.clip(jax.random.uniform(arg_keys[5], (D,), jnp.float32, -1.0, 1.0) * shard_levels(arg_keys[5], (D,), ((0, 2),), -0.4, 0.0), -1.0, 1.0)
    second_skip = jnp.clip(jax.random.uniform(arg_keys[6], (D,), jnp.float32, -1.0, 1.0) * shard_levels(arg_keys[6], (D,), ((0, 2),), -0.4, 0.0), -1.0, 1.0)
    out_weight = scatter_about(arg_keys[7], (D, D), D ** -0.5, 0.09375, ((0, 2),))
    return {"value_stream": value_stream, "first_gate": first_gate, "second_gate": second_gate, "first_filter": first_filter, "second_filter": second_filter, "first_skip": first_skip, "second_skip": second_skip, "out_weight": out_weight}


def rotation(first_index, second_index, period):
    phase_angle = ((first_index * second_index) % period).astype(jnp.float32) * (2.0 * math.pi / period)
    return jnp.cos(phase_angle), -jnp.sin(phase_angle)


def make_tables():
    coarse_rows = jnp.arange(OUTER, dtype=jnp.int32)[:, None]
    coarse_cols = jnp.arange(OUTER // 2, dtype=jnp.int32)[None, :]
    coarse_real, coarse_imag = rotation(coarse_rows, coarse_cols, OUTER)
    inner_index = jnp.arange(INNER, dtype=jnp.int32)
    inner_real, inner_imag = rotation(inner_index[:, None], inner_index[None, :], INNER)
    twist_real, twist_imag = rotation(coarse_rows, inner_index[None, :], POINTS)
    return (coarse_real.astype(jnp.bfloat16), coarse_imag.astype(jnp.bfloat16),
            inner_real.astype(jnp.bfloat16), inner_imag.astype(jnp.bfloat16), twist_real, twist_imag)


def wide_einsum(form, left, right):
    return jnp.einsum(form, left.astype(jnp.float32), right.astype(jnp.float32))


def forward(signal, tables):
    coarse_real, coarse_imag, inner_real, inner_imag, twist_real, twist_imag = tables
    channels = signal.shape[1]
    folded = signal.reshape(OUTER // 2, INNER * channels)
    part_real = jnp.dot(coarse_real, folded, preferred_element_type=jnp.float32).reshape(OUTER, INNER, channels)
    part_imag = jnp.dot(coarse_imag, folded, preferred_element_type=jnp.float32).reshape(OUTER, INNER, channels)
    turn_real = twist_real[:, :, None]
    turn_imag = twist_imag[:, :, None]
    twisted_real = (part_real * turn_real - part_imag * turn_imag).astype(jnp.bfloat16)
    twisted_imag = (part_real * turn_imag + part_imag * turn_real).astype(jnp.bfloat16)
    spec_real = wide_einsum("db,cbk->cdk", inner_real, twisted_real) - wide_einsum("db,cbk->cdk", inner_imag, twisted_imag)
    spec_imag = wide_einsum("db,cbk->cdk", inner_real, twisted_imag) + wide_einsum("db,cbk->cdk", inner_imag, twisted_real)
    return spec_real, spec_imag


def multiply(signal_spec, filter_spec):
    prod_real = (signal_spec[0] * filter_spec[0] - signal_spec[1] * filter_spec[1]).astype(jnp.bfloat16)
    prod_imag = (signal_spec[0] * filter_spec[1] + signal_spec[1] * filter_spec[0]).astype(jnp.bfloat16)
    return prod_real, prod_imag


def inverse(product, tables):
    coarse_real, coarse_imag, inner_real, inner_imag, twist_real, twist_imag = tables
    prod_real, prod_imag = product
    channels = prod_real.shape[2]
    sum_real = wide_einsum("bd,cdk->cbk", inner_real, prod_real) + wide_einsum("bd,cdk->cbk", inner_imag, prod_imag)
    sum_imag = wide_einsum("bd,cdk->cbk", inner_real, prod_imag) - wide_einsum("bd,cdk->cbk", inner_imag, prod_real)
    turn_real = twist_real[:, :, None]
    turn_imag = twist_imag[:, :, None]
    back_real = (sum_real * turn_real + sum_imag * turn_imag).astype(jnp.bfloat16)
    back_imag = (sum_imag * turn_real - sum_real * turn_imag).astype(jnp.bfloat16)
    summed = jnp.dot(coarse_real.T, back_real.reshape(OUTER, INNER * channels), preferred_element_type=jnp.float32)
    summed = summed + jnp.dot(coarse_imag.T, back_imag.reshape(OUTER, INNER * channels), preferred_element_type=jnp.float32)
    return (summed / POINTS).reshape(TOKENS, channels)


def reference(value_stream, first_gate, second_gate, first_filter, second_filter, first_skip, second_skip, out_weight):
    tables = make_tables()
    block_width = min(D, 512)
    block_count = D // block_width

    def to_blocks(array):
        return array.reshape(TOKENS, block_count, block_width).transpose(1, 0, 2)

    def mix_block(operands):
        stream_block, gate_one, gate_two, filter_one, filter_two, skip_one, skip_two = operands
        spec_one = forward(filter_one, tables)
        spec_two = forward(filter_two, tables)
        conv_one = inverse(multiply(forward(stream_block, tables), spec_one), tables)
        first_mixed = (gate_one.astype(jnp.float32) * (conv_one + skip_one * stream_block.astype(jnp.float32))).astype(jnp.bfloat16)
        conv_two = inverse(multiply(forward(first_mixed, tables), spec_two), tables)
        return (gate_two.astype(jnp.float32) * (conv_two + skip_two * first_mixed.astype(jnp.float32))).astype(jnp.bfloat16)

    mixed = lax.map(mix_block, (to_blocks(value_stream), to_blocks(first_gate), to_blocks(second_gate),
                                to_blocks(first_filter), to_blocks(second_filter),
                                first_skip.reshape(block_count, block_width), second_skip.reshape(block_count, block_width)))
    mixed = mixed.transpose(1, 0, 2).reshape(TOKENS, D)
    return jnp.dot(mixed, out_weight, preferred_element_type=jnp.float32).astype(jnp.bfloat16)
```

```python
import math

import jax
import jax.numpy as jnp
from jax import lax
from jax.sharding import PartitionSpec as P

INNER = 64


def rotation(first_index, second_index, period):
    phase_angle = (first_index * second_index % period).astype(jnp.float32) * (
        2.0 * math.pi / period
    )
    return (jnp.cos(phase_angle), -jnp.sin(phase_angle))


def make_tables(tokens):
    points = 2 * tokens
    coarse_len = points // INNER
    coarse = jnp.arange(coarse_len, dtype=jnp.int32)
    inner = jnp.arange(INNER, dtype=jnp.int32)
    coarse_real, coarse_imag = rotation(coarse[:, None], coarse[None, : coarse_len // 2], coarse_len)
    inner_real, inner_imag = rotation(inner[:, None], inner[None, :], INNER)
    twist_real, twist_imag = rotation(coarse[:, None], inner[None, :], points)
    outer = jnp.concatenate([coarse_real, coarse_imag], 0).astype(jnp.bfloat16)
    inside = jnp.concatenate(
        [
            jnp.concatenate([inner_real, -inner_imag], 1),
            jnp.concatenate([inner_imag, inner_real], 1),
        ],
        0,
    ).astype(jnp.bfloat16)
    return outer, inside, twist_real[:, :, None], twist_imag[:, :, None]


def forward(signal, tables):
    outer, inside, twist_real, twist_imag = tables
    tokens, channels = signal.shape
    part = jnp.dot(
        outer, signal.reshape(tokens // INNER, INNER * channels), preferred_element_type=jnp.float32
    ).reshape(2, -1, INNER, channels)
    twisted = jnp.concatenate(
        [
            (part[0] * twist_real - part[1] * twist_imag).astype(jnp.bfloat16),
            (part[0] * twist_imag + part[1] * twist_real).astype(jnp.bfloat16),
        ],
        axis=1,
    )
    spec = jnp.einsum("pq,cqk->cpk", inside, twisted, preferred_element_type=jnp.float32)
    return spec[:, :INNER], spec[:, INNER:]


def convolve(signal_spec, filter_spec, tables):
    outer, inside, twist_real, twist_imag = tables
    product = jnp.concatenate(
        [
            (signal_spec[0] * filter_spec[0] - signal_spec[1] * filter_spec[1]).astype(jnp.bfloat16),
            (signal_spec[0] * filter_spec[1] + signal_spec[1] * filter_spec[0]).astype(jnp.bfloat16),
        ],
        axis=1,
    )
    back = jnp.einsum("qp,cqk->cpk", inside, product, preferred_element_type=jnp.float32)
    back_real, back_imag = back[:, :INNER], back[:, INNER:]
    coarse_len, _, channels = back_real.shape
    turned = jnp.stack(
        [
            (back_real * twist_real + back_imag * twist_imag).astype(jnp.bfloat16),
            (back_imag * twist_real - back_real * twist_imag).astype(jnp.bfloat16),
        ]
    ).reshape(2 * coarse_len, INNER * channels)
    summed = lax.dot_general(
        outer, turned, (((0,), (0,)), ((), ())), preferred_element_type=jnp.float32
    )
    return (summed / (coarse_len * INNER)).reshape(-1, channels)


def shards(
    value_stream,
    first_gate,
    second_gate,
    first_filter,
    second_filter,
    first_skip,
    second_skip,
    out_weight,
):
    seq_count = lax.axis_size("seq")
    position = lax.axis_index("seq")
    tok_rows, channels = value_stream.shape
    share = channels // seq_count
    tables = make_tables(tok_rows * seq_count)

    def own_channels(field):
        return lax.all_to_all(field, "seq", split_axis=1, concat_axis=0, tiled=True)

    skip_one = lax.dynamic_slice_in_dim(first_skip, position * share, share)
    skip_two = lax.dynamic_slice_in_dim(second_skip, position * share, share)
    filter_one = own_channels(first_filter)
    value = own_channels(value_stream)
    gate_one = own_channels(first_gate)
    filter_two = own_channels(second_filter)
    conv_one = convolve(forward(value, tables), forward(filter_one, tables), tables)
    first_mixed = (
        gate_one.astype(jnp.float32) * (conv_one + skip_one * value.astype(jnp.float32))
    ).astype(jnp.bfloat16)
    conv_two = convolve(forward(first_mixed, tables), forward(filter_two, tables), tables)
    mixed = (conv_two + skip_two * first_mixed.astype(jnp.float32)).astype(jnp.bfloat16)
    rows = lax.all_to_all(mixed, "seq", split_axis=0, concat_axis=1, tiled=True)
    rows_mixed = (second_gate.astype(jnp.float32) * rows.astype(jnp.float32)).astype(jnp.bfloat16)
    partial_terms = jnp.dot(rows_mixed, out_weight, preferred_element_type=jnp.float32)
    return lax.psum_scatter(
        partial_terms.astype(jnp.bfloat16), "ch", scatter_dimension=1, tiled=True
    )


def solution(mesh):
    return jax.shard_map(
        shards,
        mesh=mesh,
        in_specs=(
            P("seq", "ch"),
            P("seq", "ch"),
            P("seq", "ch"),
            P("seq", "ch"),
            P("seq", "ch"),
            P("ch"),
            P("ch"),
            P("ch", None),
        ),
        out_specs=P("seq", "ch"),
        check_vma=False,
    )
```

```python
import math

import jax
import jax.numpy as jnp
import ml_dtypes
import numpy as np
from jax import lax
from jax.experimental import pallas as pl
from jax.experimental.pallas import tpu as pltpu
from jax.sharding import PartitionSpec as P

INNER = 64


def rotation(first_index, second_index, period):
    phase_angle = (first_index * second_index % period).astype(jnp.float32) * (
        2.0 * math.pi / period
    )
    return (jnp.cos(phase_angle), -jnp.sin(phase_angle))


def make_tables(tokens):
    points = 2 * tokens
    coarse_len = points // INNER
    coarse = jnp.arange(coarse_len, dtype=jnp.int32)
    inner = jnp.arange(INNER, dtype=jnp.int32)
    coarse_real, coarse_imag = rotation(coarse[:, None], coarse[None, : coarse_len // 2], coarse_len)
    inner_real, inner_imag = rotation(inner[:, None], inner[None, :], INNER)
    twist_real, twist_imag = rotation(coarse[:, None], inner[None, :], points)
    outer = jnp.concatenate([coarse_real, coarse_imag], 0).astype(jnp.bfloat16)
    inside = jnp.concatenate(
        [
            jnp.concatenate([inner_real, -inner_imag], 1),
            jnp.concatenate([inner_imag, inner_real], 1),
        ],
        0,
    ).astype(jnp.bfloat16)
    return outer, inside, twist_real[:, :, None], twist_imag[:, :, None]


def forward(signal, tables):
    outer, inside, twist_real, twist_imag = tables
    tokens, channels = signal.shape
    part = jnp.dot(
        outer, signal.reshape(tokens // INNER, INNER * channels), preferred_element_type=jnp.float32
    ).reshape(2, -1, INNER, channels)
    twisted = jnp.concatenate(
        [
            (part[0] * twist_real - part[1] * twist_imag).astype(jnp.bfloat16),
            (part[0] * twist_imag + part[1] * twist_real).astype(jnp.bfloat16),
        ],
        axis=1,
    )
    spec = jnp.einsum("pq,cqk->cpk", inside, twisted, preferred_element_type=jnp.float32)
    return spec[:, :INNER], spec[:, INNER:]


def convolve(signal_spec, filter_spec, tables):
    outer, inside, twist_real, twist_imag = tables
    product = jnp.concatenate(
        [
            (signal_spec[0] * filter_spec[0] - signal_spec[1] * filter_spec[1]).astype(jnp.bfloat16),
            (signal_spec[0] * filter_spec[1] + signal_spec[1] * filter_spec[0]).astype(jnp.bfloat16),
        ],
        axis=1,
    )
    back = jnp.einsum("qp,cqk->cpk", inside, product, preferred_element_type=jnp.float32)
    back_real, back_imag = back[:, :INNER], back[:, INNER:]
    coarse_len, _, channels = back_real.shape
    turned = jnp.stack(
        [
            (back_real * twist_real + back_imag * twist_imag).astype(jnp.bfloat16),
            (back_imag * twist_real - back_real * twist_imag).astype(jnp.bfloat16),
        ]
    ).reshape(2 * coarse_len, INNER * channels)
    summed = lax.dot_general(
        outer, turned, (((0,), (0,)), ((), ())), preferred_element_type=jnp.float32
    )
    return (summed / (coarse_len * INNER)).reshape(-1, channels)


def folded_tables(tokens):
    points = 2 * tokens
    coarse_len = points // INNER
    half = coarse_len // 2
    kept = half + 8
    b = np.arange(INNER)[:, None, None, None]
    c = np.arange(kept)[None, :, None, None]
    a = np.arange(half)[None, None, None, :]
    angle = (c * (INNER * a + b) % points) * (2.0 * math.pi / points)
    table = np.concatenate([np.cos(angle), -np.sin(angle)], axis=2) * (c <= half)
    weight = np.where((c == 0) | (c == half), 1.0, 2.0) / points
    forth = table.reshape(INNER, 2 * kept, half)
    back = (table * weight).reshape(INNER, 2 * kept, half).transpose(0, 2, 1)
    index = np.arange(INNER)
    angle = (index[:, None] * index[None, :] % INNER) * (2.0 * math.pi / INNER)
    real, imag = np.cos(angle), -np.sin(angle)
    inside = np.block([[real, -imag], [imag, real]])
    return tuple(jnp.asarray(t.astype(ml_dtypes.bfloat16)) for t in (forth, back, inside, inside.T))


def convolve_rows(signal, taps, forth, back, inside, outside, signal_half, taps_half, total):
    tokens, channels = signal.shape
    half = tokens // INNER
    kept2 = forth.shape[1]

    def outer(b, _):
        rows = pl.ds(b, half, stride=INNER)
        both = jnp.concatenate([signal[rows, :], taps[rows, :]], axis=1).astype(jnp.bfloat16)
        part = jnp.dot(forth[b], both, preferred_element_type=jnp.float32)
        spread = pl.ds(b, kept2, stride=INNER)
        signal_half[spread, :] = part[:, :channels]
        taps_half[spread, :] = part[:, channels:]
        return 0

    lax.fori_loop(0, INNER, outer, 0, unroll=4)

    def inner(c, _):
        rows = pl.ds(pl.multiple_of(c * 2 * INNER, 2 * INNER), 2 * INNER)
        both = jnp.concatenate([signal_half[rows, :], taps_half[rows, :]], axis=1)
        spec = jnp.dot(inside[...], both.astype(jnp.bfloat16), preferred_element_type=jnp.float32)
        sig_re, sig_im = spec[:INNER, :channels], spec[INNER:, :channels]
        tap_re, tap_im = spec[:INNER, channels:], spec[INNER:, channels:]
        product = jnp.concatenate(
            [sig_re * tap_re - sig_im * tap_im, sig_re * tap_im + sig_im * tap_re], axis=0
        ).astype(jnp.bfloat16)
        signal_half[rows, :] = jnp.dot(outside[...], product, preferred_element_type=jnp.float32)
        return 0

    lax.fori_loop(0, half + 1, inner, 0, unroll=5)

    def last(b, _):
        folded = signal_half[pl.ds(b, kept2, stride=INNER), :].astype(jnp.bfloat16)
        total[pl.ds(b, half, stride=INNER), :] = jnp.dot(
            back[b], folded, preferred_element_type=jnp.float32
        )
        return 0

    lax.fori_loop(0, INNER, last, 0, unroll=4)


def first_kernel(
    taps_ref, value_ref, skip_ref, forth, back, inside, outside, out_ref,
    signal, taps, signal_half, taps_half,
):
    signal[...] = value_ref[...].astype(jnp.float32)
    taps[...] = taps_ref[...].astype(jnp.float32)
    convolve_rows(signal, taps, forth, back, inside, outside, signal_half, taps_half, out_ref)
    out_ref[...] += skip_ref[...] * signal[...]


def second_kernel(
    taps_ref, first_ref, gate_ref, skip_ref, forth, back, inside, outside, out_ref,
    signal, taps, signal_half, taps_half, total,
):
    mixed = (gate_ref[...].astype(jnp.float32) * first_ref[...]).astype(jnp.bfloat16)
    signal[...] = mixed.astype(jnp.float32)
    taps[...] = taps_ref[...].astype(jnp.float32)
    convolve_rows(signal, taps, forth, back, inside, outside, signal_half, taps_half, total)
    out_ref[...] = (total[...] + skip_ref[...] * signal[...]).astype(jnp.bfloat16)


def call_local(kernel, dtype, tokens, channels, extra, *operands):
    kept2 = operands[-4].shape[1]
    field = pltpu.VMEM((tokens, channels), jnp.float32)
    half_field = pltpu.VMEM((kept2 * INNER, channels), jnp.float32)
    return pl.pallas_call(
        kernel,
        out_shape=jax.ShapeDtypeStruct((tokens, channels), dtype),
        in_specs=[pl.BlockSpec(memory_space=pltpu.VMEM)] * len(operands),
        out_specs=pl.BlockSpec(memory_space=pltpu.VMEM),
        scratch_shapes=[field, field, half_field, half_field] + [field] * extra,
        compiler_params=pltpu.CompilerParams(vmem_limit_bytes=48 * 1024 * 1024),
        cost_estimate=pl.CostEstimate(
            flops=16_000_000_000, bytes_accessed=8_000_000, transcendentals=0
        ),
    )(*operands)


def local_mixing(first_filter, value_stream, first_gate, second_filter, skip_one, skip_two):
    rows, channels = value_stream.shape
    seq_count = lax.axis_size("seq")
    tokens, share = rows * seq_count, channels // seq_count
    tables = folded_tables(tokens)

    def pair(one, two):
        both = jnp.stack([one, two]).reshape(2, rows, seq_count, share).transpose(2, 0, 1, 3)
        got = lax.all_to_all(both, "seq", split_axis=0, concat_axis=0, tiled=True)
        return got[:, 0].reshape(tokens, share), got[:, 1].reshape(tokens, share)

    taps_one, value = pair(first_filter, value_stream)
    gate_one, taps_two = pair(first_gate, second_filter)
    first = call_local(
        first_kernel, jnp.float32, tokens, share, 0, taps_one, value, skip_one[None, :], *tables
    )
    return call_local(
        second_kernel, jnp.bfloat16, tokens, share, 1,
        taps_two, first, gate_one, skip_two[None, :], *tables,
    )


def shards(
    value_stream,
    first_gate,
    second_gate,
    first_filter,
    second_filter,
    first_skip,
    second_skip,
    out_weight,
):
    seq_count = lax.axis_size("seq")
    position = lax.axis_index("seq")
    tok_rows, channels = value_stream.shape
    share = channels // seq_count

    def own_channels(field):
        return lax.all_to_all(field, "seq", split_axis=1, concat_axis=0, tiled=True)

    skip_one = lax.dynamic_slice_in_dim(first_skip, position * share, share)
    skip_two = lax.dynamic_slice_in_dim(second_skip, position * share, share)
    if share % 128 == 0:
        mixed = local_mixing(
            first_filter, value_stream, first_gate, second_filter, skip_one, skip_two
        )
    else:
        tables = make_tables(tok_rows * seq_count)
        filter_one = own_channels(first_filter)
        value = own_channels(value_stream)
        gate_one = own_channels(first_gate)
        filter_two = own_channels(second_filter)
        conv_one = convolve(forward(value, tables), forward(filter_one, tables), tables)
        first_mixed = (
            gate_one.astype(jnp.float32) * (conv_one + skip_one * value.astype(jnp.float32))
        ).astype(jnp.bfloat16)
        conv_two = convolve(forward(first_mixed, tables), forward(filter_two, tables), tables)
        mixed = (conv_two + skip_two * first_mixed.astype(jnp.float32)).astype(jnp.bfloat16)
    rows = lax.all_to_all(mixed, "seq", split_axis=0, concat_axis=1, tiled=True)
    rows_mixed = (second_gate.astype(jnp.float32) * rows.astype(jnp.float32)).astype(jnp.bfloat16)
    if lax.axis_size("ch") == 2:
        side = lax.axis_index("ch")
        width = out_weight.shape[1] // 2
        theirs_weight = lax.dynamic_slice_in_dim(out_weight, (1 - side) * width, width, 1)
        own_weight = lax.dynamic_slice_in_dim(out_weight, side * width, width, 1)
        theirs = jnp.dot(rows_mixed, theirs_weight, preferred_element_type=jnp.float32)
        arrived = lax.ppermute(theirs.astype(jnp.bfloat16), "ch", [(0, 1), (1, 0)])
        own = jnp.dot(rows_mixed, own_weight, preferred_element_type=jnp.float32)
        return (own + arrived.astype(jnp.float32)).astype(jnp.bfloat16)
    partial_terms = jnp.dot(rows_mixed, out_weight, preferred_element_type=jnp.float32)
    return lax.psum_scatter(
        partial_terms.astype(jnp.bfloat16), "ch", scatter_dimension=1, tiled=True
    )


def solution(mesh):
    return jax.shard_map(
        shards,
        mesh=mesh,
        in_specs=(
            P("seq", "ch"),
            P("seq", "ch"),
            P("seq", "ch"),
            P("seq", "ch"),
            P("seq", "ch"),
            P("ch"),
            P("ch"),
            P("ch", None),
        ),
        out_specs=P("seq", "ch"),
        check_vma=False,
    )
```

```python
import functools
import math

import jax
import jax.numpy as jnp
import ml_dtypes
import numpy as np
from jax import lax
from jax.experimental import pallas as pl
from jax.experimental.pallas import tpu as pltpu
from jax.sharding import PartitionSpec as P

INNER = 64


def rotation(first_index, second_index, period):
    phase_angle = (first_index * second_index % period).astype(jnp.float32) * (
        2.0 * math.pi / period
    )
    return (jnp.cos(phase_angle), -jnp.sin(phase_angle))


def make_tables(tokens):
    points = 2 * tokens
    coarse_len = points // INNER
    coarse = jnp.arange(coarse_len, dtype=jnp.int32)
    inner = jnp.arange(INNER, dtype=jnp.int32)
    coarse_real, coarse_imag = rotation(coarse[:, None], coarse[None, : coarse_len // 2], coarse_len)
    inner_real, inner_imag = rotation(inner[:, None], inner[None, :], INNER)
    twist_real, twist_imag = rotation(coarse[:, None], inner[None, :], points)
    outer = jnp.concatenate([coarse_real, coarse_imag], 0).astype(jnp.bfloat16)
    inside = jnp.concatenate(
        [
            jnp.concatenate([inner_real, -inner_imag], 1),
            jnp.concatenate([inner_imag, inner_real], 1),
        ],
        0,
    ).astype(jnp.bfloat16)
    return outer, inside, twist_real[:, :, None], twist_imag[:, :, None]


def forward(signal, tables):
    outer, inside, twist_real, twist_imag = tables
    tokens, channels = signal.shape
    part = jnp.dot(
        outer, signal.reshape(tokens // INNER, INNER * channels), preferred_element_type=jnp.float32
    ).reshape(2, -1, INNER, channels)
    twisted = jnp.concatenate(
        [
            (part[0] * twist_real - part[1] * twist_imag).astype(jnp.bfloat16),
            (part[0] * twist_imag + part[1] * twist_real).astype(jnp.bfloat16),
        ],
        axis=1,
    )
    spec = jnp.einsum("pq,cqk->cpk", inside, twisted, preferred_element_type=jnp.float32)
    return spec[:, :INNER], spec[:, INNER:]


def convolve(signal_spec, filter_spec, tables):
    outer, inside, twist_real, twist_imag = tables
    product = jnp.concatenate(
        [
            (signal_spec[0] * filter_spec[0] - signal_spec[1] * filter_spec[1]).astype(jnp.bfloat16),
            (signal_spec[0] * filter_spec[1] + signal_spec[1] * filter_spec[0]).astype(jnp.bfloat16),
        ],
        axis=1,
    )
    back = jnp.einsum("qp,cqk->cpk", inside, product, preferred_element_type=jnp.float32)
    back_real, back_imag = back[:, :INNER], back[:, INNER:]
    coarse_len, _, channels = back_real.shape
    turned = jnp.stack(
        [
            (back_real * twist_real + back_imag * twist_imag).astype(jnp.bfloat16),
            (back_imag * twist_real - back_real * twist_imag).astype(jnp.bfloat16),
        ]
    ).reshape(2 * coarse_len, INNER * channels)
    summed = lax.dot_general(
        outer, turned, (((0,), (0,)), ((), ())), preferred_element_type=jnp.float32
    )
    return (summed / (coarse_len * INNER)).reshape(-1, channels)


def folded_tables(tokens):
    points = 2 * tokens
    coarse_len = points // INNER
    half = coarse_len // 2
    kept = half + 8
    b = np.arange(INNER)[:, None, None, None]
    c = np.arange(kept)[None, :, None, None]
    a = np.arange(half)[None, None, None, :]
    angle = (c * (INNER * a + b) % points) * (2.0 * math.pi / points)
    table = np.concatenate([np.cos(angle), -np.sin(angle)], axis=2) * (c <= half)
    weight = np.where((c == 0) | (c == half), 1.0, 2.0) / points
    forth = table.reshape(INNER, 2 * kept, half)
    back = (table * weight).reshape(INNER, 2 * kept, half).transpose(0, 2, 1)
    index = np.arange(INNER)
    angle = (index[:, None] * index[None, :] % INNER) * (2.0 * math.pi / INNER)
    real, imag = np.cos(angle), -np.sin(angle)
    inside = np.block([[real, -imag], [imag, real]])
    return tuple(jnp.asarray(t.astype(ml_dtypes.bfloat16)) for t in (forth, back, inside, inside.T))


def convolve_rows(signal, taps, forth, back, inside, outside, signal_half, taps_half, total):
    tokens, channels = signal.shape
    half = tokens // INNER
    kept2 = forth.shape[1]

    def outer(b, _):
        rows = pl.ds(b, half, stride=INNER)
        both = jnp.concatenate([signal[rows, :], taps[rows, :]], axis=1).astype(jnp.bfloat16)
        part = jnp.dot(forth[b], both, preferred_element_type=jnp.float32)
        spread = pl.ds(b, kept2, stride=INNER)
        signal_half[spread, :] = part[:, :channels]
        taps_half[spread, :] = part[:, channels:]
        return 0

    lax.fori_loop(0, INNER, outer, 0, unroll=4)

    group = math.gcd(half + 1, 5)

    def inner(g, _):
        slabs = [
            pl.ds(pl.multiple_of((g * group + i) * 2 * INNER, 2 * INNER), 2 * INNER)
            for i in range(group)
        ]
        sig = jnp.concatenate([signal_half[rows, :].astype(jnp.bfloat16) for rows in slabs], axis=1)
        tap = jnp.concatenate([taps_half[rows, :].astype(jnp.bfloat16) for rows in slabs], axis=1)
        sig = jnp.dot(inside[...], sig, preferred_element_type=jnp.float32)
        tap = jnp.dot(inside[...], tap, preferred_element_type=jnp.float32)
        sig_re, sig_im = sig[:INNER], sig[INNER:]
        tap_re, tap_im = tap[:INNER], tap[INNER:]
        product = jnp.concatenate(
            [sig_re * tap_re - sig_im * tap_im, sig_re * tap_im + sig_im * tap_re], axis=0
        ).astype(jnp.bfloat16)
        result = jnp.dot(outside[...], product, preferred_element_type=jnp.float32)
        for i, rows in enumerate(slabs):
            signal_half[rows, :] = result[:, i * channels : (i + 1) * channels]
        return 0

    lax.fori_loop(0, (half + 1) // group, inner, 0)

    def last(b, _):
        folded = signal_half[pl.ds(b, kept2, stride=INNER), :].astype(jnp.bfloat16)
        total[pl.ds(b, half, stride=INNER), :] = jnp.dot(
            back[b], folded, preferred_element_type=jnp.float32
        )
        return 0

    lax.fori_loop(0, INNER, last, 0, unroll=4)


def first_kernel(
    taps_ref, value_ref, skip_ref, forth, back, inside, outside, out_ref,
    signal, taps, signal_half, taps_half,
):
    signal[...] = value_ref[...].astype(jnp.float32)
    taps[...] = taps_ref[...].astype(jnp.float32)
    convolve_rows(signal, taps, forth, back, inside, outside, signal_half, taps_half, out_ref)
    out_ref[...] += skip_ref[...] * signal[...]


def second_kernel(
    taps_ref, first_ref, gate_ref, skip_ref, forth, back, inside, outside, out_ref,
    signal, taps, signal_half, taps_half, total,
):
    mixed = (gate_ref[...].astype(jnp.float32) * first_ref[...]).astype(jnp.bfloat16)
    signal[...] = mixed.astype(jnp.float32)
    taps[...] = taps_ref[...].astype(jnp.float32)
    convolve_rows(signal, taps, forth, back, inside, outside, signal_half, taps_half, total)
    out_ref[...] = (total[...] + skip_ref[...] * signal[...]).astype(jnp.bfloat16)


def call_local(kernel, dtype, tokens, channels, extra, *operands):
    kept2 = operands[-4].shape[1]
    field = pltpu.VMEM((tokens, channels), jnp.float32)
    half_field = pltpu.VMEM((kept2 * INNER, channels), jnp.float32)
    return pl.pallas_call(
        kernel,
        out_shape=jax.ShapeDtypeStruct((tokens, channels), dtype),
        in_specs=[pl.BlockSpec(memory_space=pltpu.VMEM)] * len(operands),
        out_specs=pl.BlockSpec(memory_space=pltpu.VMEM),
        scratch_shapes=[field, field, half_field, half_field] + [field] * extra,
        compiler_params=pltpu.CompilerParams(vmem_limit_bytes=48 * 1024 * 1024),
        cost_estimate=pl.CostEstimate(
            flops=16_000_000_000, bytes_accessed=8_000_000, transcendentals=0
        ),
    )(*operands)


def local_mixing(first_filter, value_stream, first_gate, second_filter, skip_one, skip_two):
    rows, channels = value_stream.shape
    seq_count = lax.axis_size("seq")
    tokens, share = rows * seq_count, channels // seq_count
    tables = folded_tables(tokens)

    def pair(one, two):
        both = jnp.stack([one, two]).reshape(2, rows, seq_count, share).transpose(2, 0, 1, 3)
        got = lax.all_to_all(both, "seq", split_axis=0, concat_axis=0, tiled=True)
        return got[:, 0].reshape(tokens, share), got[:, 1].reshape(tokens, share)

    taps_one, value = pair(first_filter, value_stream)
    gate_one, taps_two = pair(first_gate, second_filter)
    first = call_local(
        first_kernel, jnp.float32, tokens, share, 0, taps_one, value, skip_one[None, :], *tables
    )
    return call_local(
        second_kernel, jnp.bfloat16, tokens, share, 1,
        taps_two, first, gate_one, skip_two[None, :], *tables,
    )


CHUNKS = 4
TILE = 512


def tail_kernel(
    count, mixed_ref, gate_ref, weight_ref, out_ref,
    rows, gated, weight, theirs, own, arrived,
    weight_sem, local_sem, send_sem, recv_sem, side_send, side_recv,
):
    me, side = lax.axis_index("seq"), lax.axis_index("ch")
    tok_rows, channels = gate_ref.shape
    share, piece = channels // count, tok_rows // CHUNKS
    width = out_ref.shape[1]
    stride = max(count // 2 - 1, 1)

    def weight_copy(slot, owner):
        columns = pl.ds(pl.multiple_of(owner * width, width), width)
        return pltpu.make_async_copy(
            weight_ref.at[:, columns], weight.at[slot], weight_sem.at[slot]
        )

    weight_copy(0, 1 - side).start()
    weight_copy(1, side).start()

    barrier = pltpu.get_barrier_semaphore()

    def greet(j, _):
        pl.semaphore_signal(barrier, inc=1, device_id=(lax.rem(me + j, count), side))
        return 0

    lax.fori_loop(1, count, greet, 0)
    pl.semaphore_signal(barrier, inc=1, device_id=(me, 1 - side))
    pl.semaphore_wait(barrier, count)

    def columns_of(owner):
        return pl.ds(pl.multiple_of(owner * share, share), share)

    def row_copy(q, j, target, owner):
        start = pl.multiple_of(target * tok_rows + q * piece, piece)
        return pltpu.make_async_remote_copy(
            src_ref=mixed_ref.at[pl.ds(start, piece), :],
            dst_ref=rows.at[q, :, columns_of(owner)],
            send_sem=send_sem.at[q, j],
            recv_sem=recv_sem.at[q, j],
            device_id=(target, side),
        )

    def side_copy(q):
        return pltpu.make_async_remote_copy(
            src_ref=theirs.at[q],
            dst_ref=arrived.at[q],
            send_sem=side_send.at[q],
            recv_sem=side_recv.at[q],
            device_id=(me, 1 - side),
        )

    def local_copy(q):
        start = pl.multiple_of(me * tok_rows + q * piece, piece)
        return pltpu.make_async_copy(
            mixed_ref.at[pl.ds(start, piece), :], rows.at[q, :, columns_of(me)], local_sem.at[q]
        )

    def send_chunk(q, _):
        def send(i, _):
            j = 1 + lax.rem(stride * (i + 1), count - 1)
            row_copy(q, j, lax.rem(me + j, count), me).start()
            return 0

        lax.fori_loop(0, count - 1, send, 0)
        local_copy(q).start()
        return 0

    lax.fori_loop(0, CHUNKS, send_chunk, 0)
    weight_copy(0, 1 - side).wait()
    weight_copy(1, side).wait()

    def work(q, _):
        def receive(j, _):
            row_copy(q, j, lax.rem(me + j, count), lax.rem(me + count - j, count)).wait_recv()
            return 0

        lax.fori_loop(1, count, receive, 0)
        local_copy(q).wait()
        gate_rows = pl.ds(pl.multiple_of(q * piece, piece), piece)
        gated[...] = (
            gate_ref[gate_rows, :].astype(jnp.float32) * rows[q].astype(jnp.float32)
        ).astype(jnp.bfloat16)

        def project(slot, t):
            columns = pl.ds(pl.multiple_of(t * TILE, TILE), TILE)
            return columns, jnp.dot(
                gated[...], weight[slot, :, columns], preferred_element_type=jnp.float32
            )

        def for_other(t, _):
            columns, terms = project(0, t)
            theirs[q, :, columns] = terms.astype(jnp.bfloat16)
            return 0

        def for_self(t, _):
            columns, terms = project(1, t)
            own[q, :, columns] = terms
            return 0

        lax.fori_loop(0, width // TILE, for_other, 0)
        side_copy(q).start()
        lax.fori_loop(0, width // TILE, for_self, 0)
        return 0

    lax.fori_loop(0, CHUNKS, work, 0)

    def finish(q, _):
        side_copy(q).wait_recv()
        out_rows = pl.ds(pl.multiple_of(q * piece, piece), piece)
        out_ref[out_rows, :] = (own[q] + arrived[q].astype(jnp.float32)).astype(jnp.bfloat16)
        side_copy(q).wait_send()

        def sent(j, _):
            row_copy(q, j, lax.rem(me + j, count), me).wait_send()
            return 0

        lax.fori_loop(1, count, sent, 0)
        return 0

    lax.fori_loop(0, CHUNKS, finish, 0)


def project_rows(mixed, gate, out_weight):
    count = lax.axis_size("seq")
    tok_rows, channels = gate.shape
    piece, width = tok_rows // CHUNKS, out_weight.shape[1] // 2
    in_vmem = pl.BlockSpec(memory_space=pltpu.VMEM)
    dma = pltpu.SemaphoreType.DMA
    return pl.pallas_call(
        functools.partial(tail_kernel, count),
        out_shape=jax.ShapeDtypeStruct((tok_rows, width), jnp.bfloat16),
        in_specs=[in_vmem, in_vmem, pl.BlockSpec(memory_space=pl.ANY)],
        out_specs=in_vmem,
        scratch_shapes=[
            pltpu.VMEM((CHUNKS, piece, channels), jnp.bfloat16),
            pltpu.VMEM((piece, channels), jnp.bfloat16),
            pltpu.VMEM((2, channels, width), jnp.bfloat16),
            pltpu.VMEM((CHUNKS, piece, width), jnp.bfloat16),
            pltpu.VMEM((CHUNKS, piece, width), jnp.float32),
            pltpu.VMEM((CHUNKS, piece, width), jnp.bfloat16),
            dma((2,)),
            dma((CHUNKS,)),
            dma((CHUNKS, count)),
            dma((CHUNKS, count)),
            dma((CHUNKS,)),
            dma((CHUNKS,)),
        ],
        compiler_params=pltpu.CompilerParams(
            collective_id=0, has_side_effects=True, vmem_limit_bytes=48 * 1024 * 1024
        ),
        cost_estimate=pl.CostEstimate(
            flops=2 * tok_rows * channels * 2 * width, bytes_accessed=20_000_000, transcendentals=0
        ),
    )(mixed, gate, out_weight)


def shards(
    value_stream,
    first_gate,
    second_gate,
    first_filter,
    second_filter,
    first_skip,
    second_skip,
    out_weight,
):
    seq_count = lax.axis_size("seq")
    position = lax.axis_index("seq")
    tok_rows, channels = value_stream.shape
    share = channels // seq_count

    def own_channels(field):
        return lax.all_to_all(field, "seq", split_axis=1, concat_axis=0, tiled=True)

    skip_one = lax.dynamic_slice_in_dim(first_skip, position * share, share)
    skip_two = lax.dynamic_slice_in_dim(second_skip, position * share, share)
    if share % 128 == 0:
        mixed = local_mixing(
            first_filter, value_stream, first_gate, second_filter, skip_one, skip_two
        )
        if lax.axis_size("ch") == 2:
            return project_rows(mixed, second_gate, out_weight)
    else:
        tables = make_tables(tok_rows * seq_count)
        filter_one = own_channels(first_filter)
        value = own_channels(value_stream)
        gate_one = own_channels(first_gate)
        filter_two = own_channels(second_filter)
        conv_one = convolve(forward(value, tables), forward(filter_one, tables), tables)
        first_mixed = (
            gate_one.astype(jnp.float32) * (conv_one + skip_one * value.astype(jnp.float32))
        ).astype(jnp.bfloat16)
        conv_two = convolve(forward(first_mixed, tables), forward(filter_two, tables), tables)
        mixed = (conv_two + skip_two * first_mixed.astype(jnp.float32)).astype(jnp.bfloat16)
    rows = lax.all_to_all(mixed, "seq", split_axis=0, concat_axis=1, tiled=True)
    rows_mixed = (second_gate.astype(jnp.float32) * rows.astype(jnp.float32)).astype(jnp.bfloat16)
    partial_terms = jnp.dot(rows_mixed, out_weight, preferred_element_type=jnp.float32)
    return lax.psum_scatter(
        partial_terms.astype(jnp.bfloat16), "ch", scatter_dimension=1, tiled=True
    )


def solution(mesh):
    return jax.shard_map(
        shards,
        mesh=mesh,
        in_specs=(
            P("seq", "ch"),
            P("seq", "ch"),
            P("seq", "ch"),
            P("seq", "ch"),
            P("seq", "ch"),
            P("ch"),
            P("ch"),
            P("ch", None),
        ),
        out_specs=P("seq", "ch"),
        check_vma=False,
    )
```

```python
import functools
import math

import jax
import jax.numpy as jnp
import ml_dtypes
import numpy as np
from jax import lax
from jax.experimental import pallas as pl
from jax.experimental.pallas import tpu as pltpu
from jax.sharding import PartitionSpec as P

INNER = 64


def rotation(first_index, second_index, period):
    phase_angle = (first_index * second_index % period).astype(jnp.float32) * (
        2.0 * math.pi / period
    )
    return (jnp.cos(phase_angle), -jnp.sin(phase_angle))


def make_tables(tokens):
    points = 2 * tokens
    coarse_len = points // INNER
    coarse = jnp.arange(coarse_len, dtype=jnp.int32)
    inner = jnp.arange(INNER, dtype=jnp.int32)
    coarse_real, coarse_imag = rotation(coarse[:, None], coarse[None, : coarse_len // 2], coarse_len)
    inner_real, inner_imag = rotation(inner[:, None], inner[None, :], INNER)
    twist_real, twist_imag = rotation(coarse[:, None], inner[None, :], points)
    outer = jnp.concatenate([coarse_real, coarse_imag], 0).astype(jnp.bfloat16)
    inside = jnp.concatenate(
        [
            jnp.concatenate([inner_real, -inner_imag], 1),
            jnp.concatenate([inner_imag, inner_real], 1),
        ],
        0,
    ).astype(jnp.bfloat16)
    return outer, inside, twist_real[:, :, None], twist_imag[:, :, None]


def forward(signal, tables):
    outer, inside, twist_real, twist_imag = tables
    tokens, channels = signal.shape
    part = jnp.dot(
        outer, signal.reshape(tokens // INNER, INNER * channels), preferred_element_type=jnp.float32
    ).reshape(2, -1, INNER, channels)
    twisted = jnp.concatenate(
        [
            (part[0] * twist_real - part[1] * twist_imag).astype(jnp.bfloat16),
            (part[0] * twist_imag + part[1] * twist_real).astype(jnp.bfloat16),
        ],
        axis=1,
    )
    spec = jnp.einsum("pq,cqk->cpk", inside, twisted, preferred_element_type=jnp.float32)
    return spec[:, :INNER], spec[:, INNER:]


def convolve(signal_spec, filter_spec, tables):
    outer, inside, twist_real, twist_imag = tables
    product = jnp.concatenate(
        [
            (signal_spec[0] * filter_spec[0] - signal_spec[1] * filter_spec[1]).astype(jnp.bfloat16),
            (signal_spec[0] * filter_spec[1] + signal_spec[1] * filter_spec[0]).astype(jnp.bfloat16),
        ],
        axis=1,
    )
    back = jnp.einsum("qp,cqk->cpk", inside, product, preferred_element_type=jnp.float32)
    back_real, back_imag = back[:, :INNER], back[:, INNER:]
    coarse_len, _, channels = back_real.shape
    turned = jnp.stack(
        [
            (back_real * twist_real + back_imag * twist_imag).astype(jnp.bfloat16),
            (back_imag * twist_real - back_real * twist_imag).astype(jnp.bfloat16),
        ]
    ).reshape(2 * coarse_len, INNER * channels)
    summed = lax.dot_general(
        outer, turned, (((0,), (0,)), ((), ())), preferred_element_type=jnp.float32
    )
    return (summed / (coarse_len * INNER)).reshape(-1, channels)


def folded_tables(tokens):
    points = 2 * tokens
    coarse_len = points // INNER
    half = coarse_len // 2
    kept = half + 8
    b = np.arange(INNER)[:, None, None, None]
    c = np.arange(kept)[None, :, None, None]
    a = np.arange(half)[None, None, None, :]
    angle = (c * (INNER * a + b) % points) * (2.0 * math.pi / points)
    table = np.concatenate([np.cos(angle), -np.sin(angle)], axis=2) * (c <= half)
    weight = np.where((c == 0) | (c == half), 1.0, 2.0) / points
    forth = table.reshape(INNER, 2 * kept, half)
    back = (table * weight).reshape(INNER, 2 * kept, half).transpose(0, 2, 1)
    index = np.arange(INNER)
    angle = (index[:, None] * index[None, :] % INNER) * (2.0 * math.pi / INNER)
    real, imag = np.cos(angle), -np.sin(angle)
    inside = np.block([[real, -imag], [imag, real]])
    return tuple(jnp.asarray(t.astype(ml_dtypes.bfloat16)) for t in (forth, back, inside, inside.T))


def widen(field):
    return field.astype(jnp.float32)


def outer_pass(pairs, forth):
    half = pairs[0][0].shape[0] // INNER
    kept2 = forth.shape[1]

    def outer(b, _):
        rows, spread = pl.ds(b, half, stride=INNER), pl.ds(b, kept2, stride=INNER)
        loaded = [source[rows, :] for source, _ in pairs]
        both = jnp.concatenate(loaded, axis=1) if len(pairs) > 1 else loaded[0]
        part = jnp.dot(forth[b], both.astype(jnp.bfloat16), preferred_element_type=jnp.float32)
        width = loaded[0].shape[1]
        for i, (_, result) in enumerate(pairs):
            result[spread, :] = part[:, i * width : (i + 1) * width]
        return 0

    lax.fori_loop(0, INNER, outer, 0, unroll=4)


def each_slab(half, body):
    group = math.gcd(half + 1, 5)

    def step(g, _):
        body(
            [
                pl.ds(pl.multiple_of((g * group + i) * 2 * INNER, 2 * INNER), 2 * INNER)
                for i in range(group)
            ]
        )
        return 0

    lax.fori_loop(0, (half + 1) // group, step, 0)


def inner_spectrum(half_field, slabs, inside):
    field = jnp.concatenate([half_field[rows, :].astype(jnp.bfloat16) for rows in slabs], axis=1)
    return jnp.dot(inside[...], field, preferred_element_type=jnp.float32)


def put_slabs(half_field, slabs, values):
    channels = half_field.shape[1]
    for i, rows in enumerate(slabs):
        half_field[rows, :] = values[:, i * channels : (i + 1) * channels]


def inner_pass(signal_half, taps_half, inside, outside, half, taps_done):
    def body(slabs):
        sig = inner_spectrum(signal_half, slabs, inside)
        if taps_done:
            tap = jnp.concatenate([taps_half[rows, :] for rows in slabs], axis=1)
        else:
            tap = inner_spectrum(taps_half, slabs, inside)
        sig_re, sig_im = sig[:INNER], sig[INNER:]
        tap_re, tap_im = tap[:INNER], tap[INNER:]
        product = jnp.concatenate(
            [sig_re * tap_re - sig_im * tap_im, sig_re * tap_im + sig_im * tap_re], axis=0
        ).astype(jnp.bfloat16)
        result = jnp.dot(outside[...], product, preferred_element_type=jnp.float32)
        put_slabs(signal_half, slabs, result)

    each_slab(half, body)


def last_pass(signal_half, back, total):
    half, kept2 = back.shape[1:]

    def last(b, _):
        folded = signal_half[pl.ds(b, kept2, stride=INNER), :].astype(jnp.bfloat16)
        total[pl.ds(b, half, stride=INNER), :] = jnp.dot(
            back[b], folded, preferred_element_type=jnp.float32
        )
        return 0

    lax.fori_loop(0, INNER, last, 0, unroll=4)


def mixing_kernel(
    count, taps_one_ref, value_ref, taps_two_ref, gate_ref, skip_one_ref, skip_two_ref,
    forth_ref, back_ref, inside, outside, out_ref,
    got, signal, taps, signal_half, taps_half, total, forth, back,
    table_sem, local_sem, send_sem, recv_sem,
):
    me, side = lax.axis_index("seq"), lax.axis_index("ch")
    tok_rows, channels = value_ref.shape
    share = channels // count
    half = forth_ref.shape[2]
    stride = max(count // 2 - 1, 1)
    fields = (taps_one_ref, value_ref, taps_two_ref, gate_ref)

    forth_copy = pltpu.make_async_copy(forth_ref, forth, table_sem.at[0])
    back_copy = pltpu.make_async_copy(back_ref, back, table_sem.at[1])

    barrier = pltpu.get_barrier_semaphore()

    def greet(j, _):
        pl.semaphore_signal(barrier, inc=1, device_id=(lax.rem(me + j, count), side))
        return 0

    lax.fori_loop(1, count, greet, 0)
    pl.semaphore_wait(barrier, count - 1)

    def columns_of(owner):
        return pl.ds(pl.multiple_of(owner * share, share), share)

    def rows_of(owner):
        return pl.ds(pl.multiple_of(owner * tok_rows, tok_rows), tok_rows)

    def field_copy(f, j, target, owner):
        return pltpu.make_async_remote_copy(
            src_ref=fields[f].at[:, columns_of(target)],
            dst_ref=got.at[f, rows_of(owner), :],
            send_sem=send_sem.at[f, j],
            recv_sem=recv_sem.at[f, j],
            device_id=(target, side),
        )

    def local_copy(f):
        return pltpu.make_async_copy(
            fields[f].at[:, columns_of(me)], got.at[f, rows_of(me), :], local_sem.at[f]
        )

    def send(f):
        def one(i, _):
            j = 1 + lax.rem(stride * (i + 1), count - 1)
            field_copy(f, j, lax.rem(me + j, count), me).start()
            return 0

        lax.fori_loop(0, count - 1, one, 0)
        local_copy(f).start()

    def receive(f):
        def one(j, _):
            field_copy(f, j, lax.rem(me + j, count), lax.rem(me + count - j, count)).wait_recv()
            return 0

        lax.fori_loop(1, count, one, 0)
        local_copy(f).wait()

    send(0)
    send(1)
    forth_copy.start()
    back_copy.start()
    receive(0)
    send(2)
    taps[...] = widen(got[0])
    receive(1)
    send(3)
    signal[...] = widen(got[1])
    forth_copy.wait()
    back_copy.wait()
    outer_pass([(signal, signal_half), (taps, taps_half)], forth)
    inner_pass(signal_half, taps_half, inside, outside, half, False)
    last_pass(signal_half, back, total)
    total[...] += skip_one_ref[...] * signal[...]

    receive(2)
    taps[...] = widen(got[2])
    outer_pass([(taps, taps_half)], forth)
    each_slab(
        half, lambda slabs: put_slabs(taps_half, slabs, inner_spectrum(taps_half, slabs, inside))
    )

    receive(3)
    signal[...] = widen((widen(got[3]) * total[...]).astype(jnp.bfloat16))
    outer_pass([(signal, signal_half)], forth)
    inner_pass(signal_half, taps_half, inside, outside, half, True)
    last_pass(signal_half, back, total)
    out_ref[...] = (total[...] + skip_two_ref[...] * signal[...]).astype(jnp.bfloat16)

    for f in range(len(fields)):

        def sent(j, _):
            field_copy(f, j, lax.rem(me + j, count), me).wait_send()
            return 0

        lax.fori_loop(1, count, sent, 0)


def local_mixing(first_filter, value_stream, first_gate, second_filter, skip_one, skip_two):
    rows, channels = value_stream.shape
    count = lax.axis_size("seq")
    tokens, share = rows * count, channels // count
    forth, back, inside, outside = folded_tables(tokens)
    in_vmem = pl.BlockSpec(memory_space=pltpu.VMEM)
    anywhere = pl.BlockSpec(memory_space=pl.ANY)
    dma = pltpu.SemaphoreType.DMA
    field = pltpu.VMEM((tokens, share), jnp.float32)
    half_field = pltpu.VMEM((forth.shape[1] * INNER, share), jnp.float32)
    return pl.pallas_call(
        functools.partial(mixing_kernel, count),
        out_shape=jax.ShapeDtypeStruct((tokens, share), jnp.bfloat16),
        in_specs=[anywhere] * 4 + [in_vmem] * 2 + [anywhere] * 2 + [in_vmem] * 2,
        out_specs=in_vmem,
        scratch_shapes=[
            pltpu.VMEM((4, tokens, share), jnp.bfloat16),
            field,
            field,
            half_field,
            half_field,
            field,
            pltpu.VMEM(forth.shape, jnp.bfloat16),
            pltpu.VMEM(back.shape, jnp.bfloat16),
            dma((2,)),
            dma((4,)),
            dma((4, count)),
            dma((4, count)),
        ],
        compiler_params=pltpu.CompilerParams(
            collective_id=1, has_side_effects=True, vmem_limit_bytes=48 * 1024 * 1024
        ),
        cost_estimate=pl.CostEstimate(
            flops=20_000_000_000, bytes_accessed=16_000_000, transcendentals=0
        ),
    )(
        first_filter, value_stream, second_filter, first_gate,
        skip_one[None, :], skip_two[None, :], forth, back, inside, outside,
    )


CHUNKS = 4
TILE = 512


def tail_kernel(
    count, mixed_ref, gate_ref, weight_ref, out_ref,
    rows, gated, weight, theirs, own, arrived,
    weight_sem, local_sem, send_sem, recv_sem, side_send, side_recv,
):
    me, side = lax.axis_index("seq"), lax.axis_index("ch")
    tok_rows, channels = gate_ref.shape
    share, piece = channels // count, tok_rows // CHUNKS
    width = out_ref.shape[1]
    stride = max(count // 2 - 1, 1)

    def weight_copy(slot, owner):
        columns = pl.ds(pl.multiple_of(owner * width, width), width)
        return pltpu.make_async_copy(
            weight_ref.at[:, columns], weight.at[slot], weight_sem.at[slot]
        )

    weight_copy(0, 1 - side).start()
    weight_copy(1, side).start()

    barrier = pltpu.get_barrier_semaphore()

    def greet(j, _):
        pl.semaphore_signal(barrier, inc=1, device_id=(lax.rem(me + j, count), side))
        return 0

    lax.fori_loop(1, count, greet, 0)
    pl.semaphore_signal(barrier, inc=1, device_id=(me, 1 - side))
    pl.semaphore_wait(barrier, count)

    def columns_of(owner):
        return pl.ds(pl.multiple_of(owner * share, share), share)

    def row_copy(q, j, target, owner):
        start = pl.multiple_of(target * tok_rows + q * piece, piece)
        return pltpu.make_async_remote_copy(
            src_ref=mixed_ref.at[pl.ds(start, piece), :],
            dst_ref=rows.at[q, :, columns_of(owner)],
            send_sem=send_sem.at[q, j],
            recv_sem=recv_sem.at[q, j],
            device_id=(target, side),
        )

    def side_copy(q):
        return pltpu.make_async_remote_copy(
            src_ref=theirs.at[q],
            dst_ref=arrived.at[q],
            send_sem=side_send.at[q],
            recv_sem=side_recv.at[q],
            device_id=(me, 1 - side),
        )

    def local_copy(q):
        start = pl.multiple_of(me * tok_rows + q * piece, piece)
        return pltpu.make_async_copy(
            mixed_ref.at[pl.ds(start, piece), :], rows.at[q, :, columns_of(me)], local_sem.at[q]
        )

    def send_chunk(q, _):
        def send(i, _):
            j = 1 + lax.rem(stride * (i + 1), count - 1)
            row_copy(q, j, lax.rem(me + j, count), me).start()
            return 0

        lax.fori_loop(0, count - 1, send, 0)
        local_copy(q).start()
        return 0

    lax.fori_loop(0, 2, send_chunk, 0)
    weight_copy(0, 1 - side).wait()
    weight_copy(1, side).wait()

    def work(q, _):
        def receive(j, _):
            row_copy(q, j, lax.rem(me + j, count), lax.rem(me + count - j, count)).wait_recv()
            return 0

        lax.fori_loop(1, count, receive, 0)
        local_copy(q).wait()

        @pl.when(q + 2 < CHUNKS)
        def _():
            send_chunk(q + 2, 0)

        gate_rows = pl.ds(pl.multiple_of(q * piece, piece), piece)
        gated[...] = (
            gate_ref[gate_rows, :].astype(jnp.float32) * rows[q].astype(jnp.float32)
        ).astype(jnp.bfloat16)

        def project(slot, t):
            columns = pl.ds(pl.multiple_of(t * TILE, TILE), TILE)
            return columns, jnp.dot(
                gated[...], weight[slot, :, columns], preferred_element_type=jnp.float32
            )

        def for_other(t, _):
            columns, terms = project(0, t)
            theirs[q, :, columns] = terms.astype(jnp.bfloat16)
            return 0

        def for_self(t, _):
            columns, terms = project(1, t)
            own[q, :, columns] = terms
            return 0

        lax.fori_loop(0, width // TILE, for_other, 0)
        side_copy(q).start()
        lax.fori_loop(0, width // TILE, for_self, 0)
        return 0

    lax.fori_loop(0, CHUNKS, work, 0)

    def finish(q, _):
        side_copy(q).wait_recv()
        out_rows = pl.ds(pl.multiple_of(q * piece, piece), piece)
        out_ref[out_rows, :] = (own[q] + arrived[q].astype(jnp.float32)).astype(jnp.bfloat16)
        side_copy(q).wait_send()

        def sent(j, _):
            row_copy(q, j, lax.rem(me + j, count), me).wait_send()
            return 0

        lax.fori_loop(1, count, sent, 0)
        return 0

    lax.fori_loop(0, CHUNKS, finish, 0)


def project_rows(mixed, gate, out_weight):
    count = lax.axis_size("seq")
    tok_rows, channels = gate.shape
    piece, width = tok_rows // CHUNKS, out_weight.shape[1] // 2
    in_vmem = pl.BlockSpec(memory_space=pltpu.VMEM)
    dma = pltpu.SemaphoreType.DMA
    return pl.pallas_call(
        functools.partial(tail_kernel, count),
        out_shape=jax.ShapeDtypeStruct((tok_rows, width), jnp.bfloat16),
        in_specs=[in_vmem, in_vmem, pl.BlockSpec(memory_space=pl.ANY)],
        out_specs=in_vmem,
        scratch_shapes=[
            pltpu.VMEM((CHUNKS, piece, channels), jnp.bfloat16),
            pltpu.VMEM((piece, channels), jnp.bfloat16),
            pltpu.VMEM((2, channels, width), jnp.bfloat16),
            pltpu.VMEM((CHUNKS, piece, width), jnp.bfloat16),
            pltpu.VMEM((CHUNKS, piece, width), jnp.float32),
            pltpu.VMEM((CHUNKS, piece, width), jnp.bfloat16),
            dma((2,)),
            dma((CHUNKS,)),
            dma((CHUNKS, count)),
            dma((CHUNKS, count)),
            dma((CHUNKS,)),
            dma((CHUNKS,)),
        ],
        compiler_params=pltpu.CompilerParams(
            collective_id=0, has_side_effects=True, vmem_limit_bytes=48 * 1024 * 1024
        ),
        cost_estimate=pl.CostEstimate(
            flops=2 * tok_rows * channels * 2 * width, bytes_accessed=20_000_000, transcendentals=0
        ),
    )(mixed, gate, out_weight)


def shards(
    value_stream,
    first_gate,
    second_gate,
    first_filter,
    second_filter,
    first_skip,
    second_skip,
    out_weight,
):
    seq_count = lax.axis_size("seq")
    position = lax.axis_index("seq")
    tok_rows, channels = value_stream.shape
    share = channels // seq_count

    def own_channels(field):
        return lax.all_to_all(field, "seq", split_axis=1, concat_axis=0, tiled=True)

    skip_one = lax.dynamic_slice_in_dim(first_skip, position * share, share)
    skip_two = lax.dynamic_slice_in_dim(second_skip, position * share, share)
    if share % 128 == 0:
        mixed = local_mixing(
            first_filter, value_stream, first_gate, second_filter, skip_one, skip_two
        )
        if lax.axis_size("ch") == 2:
            return project_rows(mixed, second_gate, out_weight)
    else:
        tables = make_tables(tok_rows * seq_count)
        filter_one = own_channels(first_filter)
        value = own_channels(value_stream)
        gate_one = own_channels(first_gate)
        filter_two = own_channels(second_filter)
        conv_one = convolve(forward(value, tables), forward(filter_one, tables), tables)
        first_mixed = (
            gate_one.astype(jnp.float32) * (conv_one + skip_one * value.astype(jnp.float32))
        ).astype(jnp.bfloat16)
        conv_two = convolve(forward(first_mixed, tables), forward(filter_two, tables), tables)
        mixed = (conv_two + skip_two * first_mixed.astype(jnp.float32)).astype(jnp.bfloat16)
    rows = lax.all_to_all(mixed, "seq", split_axis=0, concat_axis=1, tiled=True)
    rows_mixed = (second_gate.astype(jnp.float32) * rows.astype(jnp.float32)).astype(jnp.bfloat16)
    partial_terms = jnp.dot(rows_mixed, out_weight, preferred_element_type=jnp.float32)
    return lax.psum_scatter(
        partial_terms.astype(jnp.bfloat16), "ch", scatter_dimension=1, tiled=True
    )


def solution(mesh):
    return jax.shard_map(
        shards,
        mesh=mesh,
        in_specs=(
            P("seq", "ch"),
            P("seq", "ch"),
            P("seq", "ch"),
            P("seq", "ch"),
            P("seq", "ch"),
            P("ch"),
            P("ch"),
            P("ch", None),
        ),
        out_specs=P("seq", "ch"),
        check_vma=False,
    )
```

```python
import functools
import math

import jax
import jax.numpy as jnp
import ml_dtypes
import numpy as np
from jax import lax
from jax.experimental import pallas as pl
from jax.experimental.pallas import tpu as pltpu
from jax.sharding import PartitionSpec as P

INNER = 64


def rotation(first_index, second_index, period):
    phase_angle = (first_index * second_index % period).astype(jnp.float32) * (
        2.0 * math.pi / period
    )
    return (jnp.cos(phase_angle), -jnp.sin(phase_angle))


def make_tables(tokens):
    points = 2 * tokens
    coarse_len = points // INNER
    coarse = jnp.arange(coarse_len, dtype=jnp.int32)
    inner = jnp.arange(INNER, dtype=jnp.int32)
    coarse_real, coarse_imag = rotation(coarse[:, None], coarse[None, : coarse_len // 2], coarse_len)
    inner_real, inner_imag = rotation(inner[:, None], inner[None, :], INNER)
    twist_real, twist_imag = rotation(coarse[:, None], inner[None, :], points)
    outer = jnp.concatenate([coarse_real, coarse_imag], 0).astype(jnp.bfloat16)
    inside = jnp.concatenate(
        [
            jnp.concatenate([inner_real, -inner_imag], 1),
            jnp.concatenate([inner_imag, inner_real], 1),
        ],
        0,
    ).astype(jnp.bfloat16)
    return outer, inside, twist_real[:, :, None], twist_imag[:, :, None]


def forward(signal, tables):
    outer, inside, twist_real, twist_imag = tables
    tokens, channels = signal.shape
    part = jnp.dot(
        outer, signal.reshape(tokens // INNER, INNER * channels), preferred_element_type=jnp.float32
    ).reshape(2, -1, INNER, channels)
    twisted = jnp.concatenate(
        [
            (part[0] * twist_real - part[1] * twist_imag).astype(jnp.bfloat16),
            (part[0] * twist_imag + part[1] * twist_real).astype(jnp.bfloat16),
        ],
        axis=1,
    )
    spec = jnp.einsum("pq,cqk->cpk", inside, twisted, preferred_element_type=jnp.float32)
    return spec[:, :INNER], spec[:, INNER:]


def convolve(signal_spec, filter_spec, tables):
    outer, inside, twist_real, twist_imag = tables
    product = jnp.concatenate(
        [
            (signal_spec[0] * filter_spec[0] - signal_spec[1] * filter_spec[1]).astype(jnp.bfloat16),
            (signal_spec[0] * filter_spec[1] + signal_spec[1] * filter_spec[0]).astype(jnp.bfloat16),
        ],
        axis=1,
    )
    back = jnp.einsum("qp,cqk->cpk", inside, product, preferred_element_type=jnp.float32)
    back_real, back_imag = back[:, :INNER], back[:, INNER:]
    coarse_len, _, channels = back_real.shape
    turned = jnp.stack(
        [
            (back_real * twist_real + back_imag * twist_imag).astype(jnp.bfloat16),
            (back_imag * twist_real - back_real * twist_imag).astype(jnp.bfloat16),
        ]
    ).reshape(2 * coarse_len, INNER * channels)
    summed = lax.dot_general(
        outer, turned, (((0,), (0,)), ((), ())), preferred_element_type=jnp.float32
    )
    return (summed / (coarse_len * INNER)).reshape(-1, channels)


def folded_tables(tokens):
    points = 2 * tokens
    coarse_len = points // INNER
    half = coarse_len // 2
    kept = half + 8
    b = np.arange(INNER)[:, None, None, None]
    c = np.arange(kept)[None, :, None, None]
    a = np.arange(half)[None, None, None, :]
    angle = (c * (INNER * a + b) % points) * (2.0 * math.pi / points)
    table = np.concatenate([np.cos(angle), -np.sin(angle)], axis=2) * (c <= half)
    weight = np.where((c == 0) | (c == half), 1.0, 2.0) / points
    forth = table.reshape(INNER, 2 * kept, half)
    back = (table * weight).reshape(INNER, 2 * kept, half).transpose(0, 2, 1)
    index = np.arange(INNER)
    angle = (index[:, None] * index[None, :] % INNER) * (2.0 * math.pi / INNER)
    real, imag = np.cos(angle), -np.sin(angle)
    inside = np.block([[real, -imag], [imag, real]])
    return tuple(jnp.asarray(t.astype(ml_dtypes.bfloat16)) for t in (forth, back, inside, inside.T))


def widen(field):
    return field.astype(jnp.float32)


def outer_pass(pairs, forth):
    half = pairs[0][0].shape[0] // INNER
    kept2 = forth.shape[1]

    def outer(b, _):
        rows, spread = pl.ds(b, half, stride=INNER), pl.ds(b, kept2, stride=INNER)
        loaded = [source[rows, :] for source, _ in pairs]
        both = jnp.concatenate(loaded, axis=1) if len(pairs) > 1 else loaded[0]
        part = jnp.dot(forth[b], both.astype(jnp.bfloat16), preferred_element_type=jnp.float32)
        width = loaded[0].shape[1]
        for i, (_, result) in enumerate(pairs):
            result[spread, :] = part[:, i * width : (i + 1) * width]
        return 0

    lax.fori_loop(0, INNER, outer, 0, unroll=4)


def each_slab(half, body):
    group = math.gcd(half + 1, 5)

    def step(g, _):
        body(
            [
                pl.ds(pl.multiple_of((g * group + i) * 2 * INNER, 2 * INNER), 2 * INNER)
                for i in range(group)
            ]
        )
        return 0

    lax.fori_loop(0, (half + 1) // group, step, 0)


def inner_spectrum(half_field, slabs, inside):
    field = jnp.concatenate([half_field[rows, :].astype(jnp.bfloat16) for rows in slabs], axis=1)
    return jnp.dot(inside[...], field, preferred_element_type=jnp.float32)


def put_slabs(half_field, slabs, values):
    channels = half_field.shape[1]
    for i, rows in enumerate(slabs):
        half_field[rows, :] = values[:, i * channels : (i + 1) * channels]


def inner_pass(signal_half, taps_half, inside, outside, half, taps_done):
    def body(slabs):
        sig = inner_spectrum(signal_half, slabs, inside)
        if taps_done:
            tap = jnp.concatenate([taps_half[rows, :] for rows in slabs], axis=1)
        else:
            tap = inner_spectrum(taps_half, slabs, inside)
        sig_re, sig_im = sig[:INNER], sig[INNER:]
        tap_re, tap_im = tap[:INNER], tap[INNER:]
        product = jnp.concatenate(
            [sig_re * tap_re - sig_im * tap_im, sig_re * tap_im + sig_im * tap_re], axis=0
        ).astype(jnp.bfloat16)
        result = jnp.dot(outside[...], product, preferred_element_type=jnp.float32)
        put_slabs(signal_half, slabs, result)

    each_slab(half, body)


def last_pass(signal_half, back, total):
    half, kept2 = back.shape[1:]

    def last(b, _):
        folded = signal_half[pl.ds(b, kept2, stride=INNER), :].astype(jnp.bfloat16)
        total[pl.ds(b, half, stride=INNER), :] = jnp.dot(
            back[b], folded, preferred_element_type=jnp.float32
        )
        return 0

    lax.fori_loop(0, INNER, last, 0, unroll=4)


def mixing_kernel(
    count, taps_one_ref, value_ref, taps_two_ref, gate_ref, skip_one_ref, skip_two_ref,
    forth_ref, back_ref, inside, outside, out_ref,
    got, signal, taps, signal_half, taps_half, total, forth, back,
    table_sem, local_sem, send_sem, recv_sem,
):
    me, side = lax.axis_index("seq"), lax.axis_index("ch")
    tok_rows, channels = value_ref.shape
    share = channels // count
    half = forth_ref.shape[2]
    stride = max(count // 2 - 1, 1)
    fields = (taps_one_ref, value_ref, taps_two_ref, gate_ref)

    forth_copy = pltpu.make_async_copy(forth_ref, forth, table_sem.at[0])
    back_copy = pltpu.make_async_copy(back_ref, back, table_sem.at[1])

    barrier = pltpu.get_barrier_semaphore()

    def greet(j, _):
        pl.semaphore_signal(barrier, inc=1, device_id=(lax.rem(me + j, count), side))
        return 0

    lax.fori_loop(1, count, greet, 0)
    pl.semaphore_wait(barrier, count - 1)

    def columns_of(owner):
        return pl.ds(pl.multiple_of(owner * share, share), share)

    def rows_of(owner):
        return pl.ds(pl.multiple_of(owner * tok_rows, tok_rows), tok_rows)

    def field_copy(f, j, target, owner):
        return pltpu.make_async_remote_copy(
            src_ref=fields[f].at[:, columns_of(target)],
            dst_ref=got.at[f, rows_of(owner), :],
            send_sem=send_sem.at[f, j],
            recv_sem=recv_sem.at[f, j],
            device_id=(target, side),
        )

    def local_copy(f):
        return pltpu.make_async_copy(
            fields[f].at[:, columns_of(me)], got.at[f, rows_of(me), :], local_sem.at[f]
        )

    def send(f):
        def one(i, _):
            j = 1 + lax.rem(stride * (i + 1), count - 1)
            field_copy(f, j, lax.rem(me + j, count), me).start()
            return 0

        lax.fori_loop(0, count - 1, one, 0)
        local_copy(f).start()

    def receive(f):
        def one(j, _):
            field_copy(f, j, lax.rem(me + j, count), lax.rem(me + count - j, count)).wait_recv()
            return 0

        lax.fori_loop(1, count, one, 0)
        local_copy(f).wait()

    send(0)
    send(1)
    forth_copy.start()
    back_copy.start()
    receive(0)
    send(2)
    taps[...] = widen(got[0])
    receive(1)
    send(3)
    signal[...] = widen(got[1])
    forth_copy.wait()
    back_copy.wait()
    outer_pass([(signal, signal_half), (taps, taps_half)], forth)
    inner_pass(signal_half, taps_half, inside, outside, half, False)
    last_pass(signal_half, back, total)
    total[...] += skip_one_ref[...] * signal[...]

    receive(2)
    taps[...] = widen(got[2])
    outer_pass([(taps, taps_half)], forth)
    each_slab(
        half, lambda slabs: put_slabs(taps_half, slabs, inner_spectrum(taps_half, slabs, inside))
    )

    receive(3)
    signal[...] = widen((widen(got[3]) * total[...]).astype(jnp.bfloat16))
    outer_pass([(signal, signal_half)], forth)
    inner_pass(signal_half, taps_half, inside, outside, half, True)
    last_pass(signal_half, back, total)
    out_ref[...] = (total[...] + skip_two_ref[...] * signal[...]).astype(jnp.bfloat16)

    for f in range(len(fields)):

        def sent(j, _):
            field_copy(f, j, lax.rem(me + j, count), me).wait_send()
            return 0

        lax.fori_loop(1, count, sent, 0)


def local_mixing(first_filter, value_stream, first_gate, second_filter, skip_one, skip_two):
    rows, channels = value_stream.shape
    count = lax.axis_size("seq")
    tokens, share = rows * count, channels // count
    forth, back, inside, outside = folded_tables(tokens)
    in_vmem = pl.BlockSpec(memory_space=pltpu.VMEM)
    anywhere = pl.BlockSpec(memory_space=pl.ANY)
    dma = pltpu.SemaphoreType.DMA
    field = pltpu.VMEM((tokens, share), jnp.float32)
    half_field = pltpu.VMEM((forth.shape[1] * INNER, share), jnp.float32)
    return pl.pallas_call(
        functools.partial(mixing_kernel, count),
        out_shape=jax.ShapeDtypeStruct((tokens, share), jnp.bfloat16),
        in_specs=[anywhere] * 4 + [in_vmem] * 2 + [anywhere] * 2 + [in_vmem] * 2,
        out_specs=in_vmem,
        scratch_shapes=[
            pltpu.VMEM((4, tokens, share), jnp.bfloat16),
            field,
            field,
            half_field,
            half_field,
            field,
            pltpu.VMEM(forth.shape, jnp.bfloat16),
            pltpu.VMEM(back.shape, jnp.bfloat16),
            dma((2,)),
            dma((4,)),
            dma((4, count)),
            dma((4, count)),
        ],
        compiler_params=pltpu.CompilerParams(
            collective_id=1, has_side_effects=True, vmem_limit_bytes=60 * 1024 * 1024
        ),
        cost_estimate=pl.CostEstimate(
            flops=20_000_000_000, bytes_accessed=16_000_000, transcendentals=0
        ),
    )(
        first_filter, value_stream, second_filter, first_gate,
        skip_one[None, :], skip_two[None, :], forth, back, inside, outside,
    )


CHUNKS = 2
TILE = 512


def tail_kernel(
    count, mixed_ref, gate_ref, weight_ref, out_ref,
    rows, gated, weight, theirs, own, arrived,
    weight_sem, local_sem, send_sem, recv_sem, side_send, side_recv,
):
    me, side = lax.axis_index("seq"), lax.axis_index("ch")
    tok_rows, channels = gate_ref.shape
    share, piece = channels // count, tok_rows // CHUNKS
    width = out_ref.shape[1]
    stride = max(count // 2 - 1, 1)

    def weight_copy(slot, owner):
        columns = pl.ds(pl.multiple_of(owner * width, width), width)
        return pltpu.make_async_copy(
            weight_ref.at[:, columns], weight.at[slot], weight_sem.at[slot]
        )

    weight_copy(0, 1 - side).start()
    weight_copy(1, side).start()

    barrier = pltpu.get_barrier_semaphore()

    def greet(j, _):
        pl.semaphore_signal(barrier, inc=1, device_id=(lax.rem(me + j, count), side))
        return 0

    lax.fori_loop(1, count, greet, 0)
    pl.semaphore_signal(barrier, inc=1, device_id=(me, 1 - side))
    pl.semaphore_wait(barrier, count)

    def columns_of(owner):
        return pl.ds(pl.multiple_of(owner * share, share), share)

    def row_copy(q, j, target, owner):
        start = pl.multiple_of(target * tok_rows + q * piece, piece)
        return pltpu.make_async_remote_copy(
            src_ref=mixed_ref.at[pl.ds(start, piece), :],
            dst_ref=rows.at[q, :, columns_of(owner)],
            send_sem=send_sem.at[q, j],
            recv_sem=recv_sem.at[q, j],
            device_id=(target, side),
        )

    def side_copy(q, t):
        columns = pl.ds(pl.multiple_of(t * TILE, TILE), TILE)
        return pltpu.make_async_remote_copy(
            src_ref=theirs.at[q, :, columns],
            dst_ref=arrived.at[q, :, columns],
            send_sem=side_send.at[q, t],
            recv_sem=side_recv.at[q, t],
            device_id=(me, 1 - side),
        )

    def local_copy(q):
        start = pl.multiple_of(me * tok_rows + q * piece, piece)
        return pltpu.make_async_copy(
            mixed_ref.at[pl.ds(start, piece), :], rows.at[q, :, columns_of(me)], local_sem.at[q]
        )

    def send_chunk(q, _):
        def send(i, _):
            j = 1 + lax.rem(stride * (i + 1), count - 1)
            row_copy(q, j, lax.rem(me + j, count), me).start()
            return 0

        lax.fori_loop(0, count - 1, send, 0)
        local_copy(q).start()
        return 0

    lax.fori_loop(0, CHUNKS, send_chunk, 0)
    weight_copy(0, 1 - side).wait()
    weight_copy(1, side).wait()

    def work(q, _):
        def receive(j, _):
            row_copy(q, j, lax.rem(me + j, count), lax.rem(me + count - j, count)).wait_recv()
            return 0

        lax.fori_loop(1, count, receive, 0)
        local_copy(q).wait()

        gate_rows = pl.ds(pl.multiple_of(q * piece, piece), piece)
        gated[...] = (
            gate_ref[gate_rows, :].astype(jnp.float32) * rows[q].astype(jnp.float32)
        ).astype(jnp.bfloat16)

        def project(slot, t):
            columns = pl.ds(pl.multiple_of(t * TILE, TILE), TILE)
            return columns, jnp.dot(
                gated[...], weight[slot, :, columns], preferred_element_type=jnp.float32
            )

        def for_other(t, _):
            columns, terms = project(0, t)
            theirs[q, :, columns] = terms.astype(jnp.bfloat16)
            side_copy(q, t).start()
            return 0

        def for_self(t, _):
            columns, terms = project(1, t)
            own[q, :, columns] = terms
            return 0

        lax.fori_loop(0, width // TILE, for_other, 0)
        lax.fori_loop(0, width // TILE, for_self, 0)
        return 0

    lax.fori_loop(0, CHUNKS, work, 0)

    def finish(q, _):
        out_rows = pl.ds(pl.multiple_of(q * piece, piece), piece)

        def add(t, _):
            side_copy(q, t).wait_recv()
            columns = pl.ds(pl.multiple_of(t * TILE, TILE), TILE)
            out_ref[out_rows, columns] = (
                own[q, :, columns] + arrived[q, :, columns].astype(jnp.float32)
            ).astype(jnp.bfloat16)
            side_copy(q, t).wait_send()
            return 0

        lax.fori_loop(0, width // TILE, add, 0)

        def sent(j, _):
            row_copy(q, j, lax.rem(me + j, count), me).wait_send()
            return 0

        lax.fori_loop(1, count, sent, 0)
        return 0

    lax.fori_loop(0, CHUNKS, finish, 0)


def project_rows(mixed, gate, out_weight):
    count = lax.axis_size("seq")
    tok_rows, channels = gate.shape
    piece, width = tok_rows // CHUNKS, out_weight.shape[1] // 2
    in_vmem = pl.BlockSpec(memory_space=pltpu.VMEM)
    dma = pltpu.SemaphoreType.DMA
    return pl.pallas_call(
        functools.partial(tail_kernel, count),
        out_shape=jax.ShapeDtypeStruct((tok_rows, width), jnp.bfloat16),
        in_specs=[in_vmem, in_vmem, pl.BlockSpec(memory_space=pl.ANY)],
        out_specs=in_vmem,
        scratch_shapes=[
            pltpu.VMEM((CHUNKS, piece, channels), jnp.bfloat16),
            pltpu.VMEM((piece, channels), jnp.bfloat16),
            pltpu.VMEM((2, channels, width), jnp.bfloat16),
            pltpu.VMEM((CHUNKS, piece, width), jnp.bfloat16),
            pltpu.VMEM((CHUNKS, piece, width), jnp.float32),
            pltpu.VMEM((CHUNKS, piece, width), jnp.bfloat16),
            dma((2,)),
            dma((CHUNKS,)),
            dma((CHUNKS, count)),
            dma((CHUNKS, count)),
            dma((CHUNKS, width // TILE)),
            dma((CHUNKS, width // TILE)),
        ],
        compiler_params=pltpu.CompilerParams(
            collective_id=0, has_side_effects=True, vmem_limit_bytes=48 * 1024 * 1024
        ),
        cost_estimate=pl.CostEstimate(
            flops=2 * tok_rows * channels * 2 * width, bytes_accessed=20_000_000, transcendentals=0
        ),
    )(mixed, gate, out_weight)


def shards(
    value_stream,
    first_gate,
    second_gate,
    first_filter,
    second_filter,
    first_skip,
    second_skip,
    out_weight,
):
    seq_count = lax.axis_size("seq")
    position = lax.axis_index("seq")
    tok_rows, channels = value_stream.shape
    share = channels // seq_count

    def own_channels(field):
        return lax.all_to_all(field, "seq", split_axis=1, concat_axis=0, tiled=True)

    skip_one = lax.dynamic_slice_in_dim(first_skip, position * share, share)
    skip_two = lax.dynamic_slice_in_dim(second_skip, position * share, share)
    if share % 128 == 0:
        mixed = local_mixing(
            first_filter, value_stream, first_gate, second_filter, skip_one, skip_two
        )
        if lax.axis_size("ch") == 2:
            return project_rows(mixed, second_gate, out_weight)
    else:
        tables = make_tables(tok_rows * seq_count)
        filter_one = own_channels(first_filter)
        value = own_channels(value_stream)
        gate_one = own_channels(first_gate)
        filter_two = own_channels(second_filter)
        conv_one = convolve(forward(value, tables), forward(filter_one, tables), tables)
        first_mixed = (
            gate_one.astype(jnp.float32) * (conv_one + skip_one * value.astype(jnp.float32))
        ).astype(jnp.bfloat16)
        conv_two = convolve(forward(first_mixed, tables), forward(filter_two, tables), tables)
        mixed = (conv_two + skip_two * first_mixed.astype(jnp.float32)).astype(jnp.bfloat16)
    rows = lax.all_to_all(mixed, "seq", split_axis=0, concat_axis=1, tiled=True)
    rows_mixed = (second_gate.astype(jnp.float32) * rows.astype(jnp.float32)).astype(jnp.bfloat16)
    partial_terms = jnp.dot(rows_mixed, out_weight, preferred_element_type=jnp.float32)
    return lax.psum_scatter(
        partial_terms.astype(jnp.bfloat16), "ch", scatter_dimension=1, tiled=True
    )


def solution(mesh):
    return jax.shard_map(
        shards,
        mesh=mesh,
        in_specs=(
            P("seq", "ch"),
            P("seq", "ch"),
            P("seq", "ch"),
            P("seq", "ch"),
            P("seq", "ch"),
            P("ch"),
            P("ch"),
            P("ch", None),
        ),
        out_specs=P("seq", "ch"),
        check_vma=False,
    )
```
